256 devices in a mesh: grp: 2 (over z_hi), own: 128 (over z_lo, y, x, core).
Axes of the slice: x: 4, y: 4, z: 8 (z_hi: 2, z_lo: 4; z = z_hi * 4 + z_lo), core: 2. Of those that a mesh axis runs over, the one named last changes fastest.
Arguments:
- points: bfloat16 [131072, 768], P(('grp', 'own')), may hold values from -6 to 6
- list_ids: int32 [131072], P(('grp', 'own')), may hold values from 0 to 65535, as said below
- code_ids: int32 [131072, 96], P(('grp', 'own')), may hold values from 0 to 255
- list_home: int32 [65536], replicated, may hold values from 0 to 65535, as said below
- centroids: bfloat16 [65536, 768], P('own'), may hold values from -3 to 3
- rotation: bfloat16 [768, 768], replicated, may hold values from -0.21875 to 0.21875
- codebook: bfloat16 [96, 8, 256], replicated, may hold values from -6 to 6
Outputs:
- encoded_rows: bfloat16 [262144, 768], P(('grp', 'own'))
- new_codebook: float32 [96, 8, 256], replicated
- procrustes_gram: float32 [768, 768], replicated
The draws below stay inside these ranges and needn't reach their ends.
Inputs may be any that keep to these rules, and one draw needn't show every extreme that they name: Within the 512 rows of one device, at most 8 rows have list_home[list_ids] // 512 equal to one value; in every draw one value is reached by exactly 8 rows on every device. `list_home`: each value occurs once.
All inputs are finite; a program needn't handle non-finite values.
Results may differ from the reference program's by a relative error of at most 0.0051.
Values may be sent and summed in bfloat16 or wider, within the bound.
A program may use at most 64 MiB of HBM per device.

```python
import math
import jax
import jax.numpy as jnp
import numpy as np
from jax import lax

D = 768
SUB = 8
M = 96
K = 256
LPD = 512
ROWS = 512
LISTS = 65536
CAP = 8
SLOTS = 1024
TOKENS = 131072
N_GRP = 2
N_OWN = 128
DEVICES = 256


def shared_home(key):
    return jax.random.permutation(jax.random.fold_in(key, 11), LISTS).astype(jnp.int32)


def draw_list_home(key, part):
    return shared_home(key)


def draw_list_ids(key, part):
    home_table = shared_home(key)
    inverse = jnp.zeros((LISTS,), jnp.int32).at[home_table].set(jnp.arange(LISTS, dtype=jnp.int32))
    key = jax.random.fold_in(key, 5)
    owners = LISTS // LPD
    blocks = TOKENS // ROWS
    hot_key, spread_key, pick_key = jax.random.split(key, 3)
    hot_owner = jax.random.randint(hot_key, (), 0, owners).astype(jnp.int32)
    slot_index = jnp.arange(ROWS, dtype=jnp.int32)

    def one_block(block_key):
        first_key, second_key = jax.random.split(block_key)
        others = jax.random.permutation(first_key, owners - 1).astype(jnp.int32)
        others = jnp.where(others >= hot_owner, others + 1, others)
        cycled = others[jnp.maximum(slot_index - CAP, 0) % (owners - 1)]
        target = jnp.where(slot_index < CAP, hot_owner, cycled)
        return target[jax.random.permutation(second_key, ROWS)]
    target = jax.vmap(one_block)(jax.random.split(spread_key, blocks))
    local_pick = jax.random.randint(pick_key, (blocks, ROWS), 0, LPD).astype(jnp.int32)
    return inverse[target * LPD + local_pick].reshape(TOKENS).astype(jnp.int32)


def set_ends(result, own_key, smallest, top_value):
    longest = result.shape.index(max(result.shape))
    spots = []
    for shift in (0, 1):
        where = [jax.random.randint(jax.random.fold_in(own_key, axis), (), 0, length) for axis, length in enumerate(result.shape)]
        where[longest] = (where[longest] + shift) % result.shape[longest]
        spots.append(tuple(where))
    return result.at[spots[0]].set(smallest).at[spots[1]].set(top_value)


def shard_levels(own_key, dims, pieces, low, high):
    level, own = 1.0, jax.random.fold_in(own_key, 6)
    for dim, parts in pieces:
        steps = jnp.exp(jax.random.uniform(jax.random.fold_in(own, dim), (parts,), jnp.float32, low / len(pieces), high / len(pieces)))
        level = level * jnp.repeat(steps, dims[dim] // parts).reshape([-1 if axis == dim else 1 for axis in range(len(dims))])
    return level


def rank_table(count, lean):
    weights = [(1 << 20) // math.isqrt(grade ** lean) + 1 for grade in range(1, count + 1)]
    width = 1 + sum(weights) // (1 << 30)
    return np.cumsum(np.array([max(1, weight // width) for weight in weights]))


def skewed_ids(own_key, extent, amount, lean):
    table = rank_table(amount, lean)
    lot = jax.random.randint(jax.random.fold_in(own_key, 1), extent, 0, int(table[amount - 1]))
    standing = jnp.searchsorted(jnp.asarray(table, jnp.int32), lot, side="right")
    return jax.random.permutation(jax.random.fold_in(own_key, 2), amount)[standing].astype(jnp.int32)


def normal_values(stream_key, dims, width, most, cuts=(), kind=jnp.bfloat16):
    array = width * jax.random.normal(stream_key, dims, jnp.float32)
    if cuts:
        array = array * shard_levels(stream_key, dims, cuts, -0.22, 0.18)
    return jnp.clip(array, -most, most).astype(kind)


def setup_inputs(seed: int = 0) -> dict:
    key_list = jax.random.split(jax.random.key(seed), 8)
    return {
        "points": normal_values(key_list[0], (TOKENS, D), 1.0, 6.0, ((0, 256),)),
        "list_ids": draw_list_ids(jax.random.fold_in(key_list[7], 71), 0),
        "code_ids": set_ends(skewed_ids(key_list[2], (TOKENS, M), K, 2), jax.random.fold_in(key_list[2], 3), 0, K - 1).astype(jnp.int32),
        "list_home": draw_list_home(jax.random.fold_in(key_list[7], 71), 0),
        "centroids": normal_values(key_list[4], (LISTS, D), 0.5, 3.0, ((0, 128),)),
        "rotation": normal_values(key_list[5], (D, D), D ** -0.5, 0.21875),
        "codebook": normal_values(key_list[6], (M, SUB, K), 1.0, 6.0),
    }


def reference(points, list_ids, code_ids, list_home, centroids, rotation, codebook):
    storage = list_home[list_ids]
    residual = (points.astype(jnp.float32) - centroids[storage].astype(jnp.float32)).astype(jnp.bfloat16)
    encoded = jnp.dot(residual, rotation, preferred_element_type=jnp.float32).astype(jnp.bfloat16)
    target = (storage // LPD).reshape(N_GRP, N_OWN, ROWS)
    matches = (target[..., None] == jnp.arange(N_OWN, dtype=jnp.int32)).astype(jnp.int32)
    position = lax.optimization_barrier(jnp.sum(jnp.cumsum(matches, axis=2) * matches, axis=3)) - 1
    group_index = jnp.arange(N_GRP, dtype=jnp.int32)[:, None, None]
    source_index = jnp.arange(N_OWN, dtype=jnp.int32)[None, :, None]
    placed = ((group_index * N_OWN + target) * N_OWN + source_index) * CAP + position
    encoded_rows = jnp.zeros((DEVICES * SLOTS, D), jnp.bfloat16).at[placed.reshape(-1).astype(jnp.int32)].set(encoded)
    book_table = jnp.transpose(codebook, (0, 2, 1))
    rebuilt = book_table[jnp.arange(M, dtype=jnp.int32)[None, :], code_ids].reshape(TOKENS, D)
    gram_sum = lax.dot_general(residual, rebuilt, (((0,), (0,)), ((), ())), preferred_element_type=jnp.float32)
    procrustes_gram = gram_sum / math.sqrt(TOKENS)
    segment_ids = (code_ids + K * jnp.arange(M, dtype=jnp.int32)[None, :]).reshape(-1)
    flat_values = encoded.astype(jnp.float32).reshape(TOKENS * M, SUB)
    code_sums = jax.ops.segment_sum(flat_values, segment_ids, num_segments=M * K).reshape(M, K, SUB)
    code_sums = jnp.transpose(code_sums, (0, 2, 1))
    code_counts = jax.ops.segment_sum(jnp.ones((TOKENS * M,), jnp.float32), segment_ids, num_segments=M * K).reshape(M, K)
    new_codebook = (code_sums + codebook.astype(jnp.float32)) / (code_counts[:, None, :] + 1.0)
    return (encoded_rows, new_codebook, procrustes_gram)
```

```python
import math

import jax
import jax.numpy as jnp
from jax import lax
from jax.experimental import pallas as pl
from jax.experimental.pallas import tpu as pltpu
from jax.sharding import PartitionSpec as P

MESH = pl.DeviceIdType.MESH
F32 = jnp.float32
BF16 = jnp.bfloat16
I32 = jnp.int32

NZ, NY, NX = 8, 4, 4
OWN = 128
CAP = 8
ROWS = 512
D = 768
M = 96
SLOTS = OWN * CAP
Q = 48
ROW_CHUNKS = 4


def dot(a, b, dims):
    return lax.dot_general(a, b, (dims, ((), ())), preferred_element_type=F32)


def nn(a, b):
    return dot(a, b, ((1,), (0,)))


def nt(a, b):
    return dot(a, b, ((1,), (1,)))


def tn(a, b):
    return dot(a, b, ((0,), (0,)))


def tt(a, b):
    return dot(a, b, ((0,), (1,)))


def iota(shape, axis):
    return lax.broadcasted_iota(I32, shape, axis)


def kernel(
    points, ids, code_ids, home, centroids, rotation, codebook,
    enc_out, book_out, gram_out,
    srow, rrow, scode, rcode, slot_s, pcodes, ccodes, ehi, elo, reb, crt_hi, crt_lo,
    centre, onel, local_s, gram, sums, counts,
    s0g, s0s, r0g, r0s, s1g, s1s, r1g, r1s, s2g, s2s, r2g, r2s, s3g, s3s, r3g, r3s,
    fin, a4, a5g, a5s, a6g, a6s, a7g, a7s,
    code_send, code_recv, row_send, row_recv, red_send, red_recv, sem_a, sem_b, own_sem,
):
    me = lax.axis_index("own")
    z = lax.axis_index("grp") * 4 + me // 32
    zl = me // 32
    y = (me // 8) % 4
    x = (me // 2) % 4
    c = me % 2
    other = 1 - c

    def at(z_, y_, x_, c_):
        return {"grp": z_ // 4, "own": (z_ % 4) * 32 + y_ * 8 + x_ * 2 + c_}

    line_x = [at(z, y, (x + d) % 4, (c + e) % 2) for d in range(4) for e in range(2) if d or e]
    line_y = [at(z, (y + d) % 4, x, c) for d in range(1, 4)]
    line_z = [at((z + d) % 8, y, x, c) for d in range(1, 8)]
    barrier = pltpu.get_barrier_semaphore()
    for peer in line_x + line_y + line_z:
        pl.semaphore_signal(barrier, inc=1, device_id=peer, device_id_type=MESH)

    row_id = ids[...]
    id_hi = lax.shift_right_logical(row_id, 7)
    id_lo = row_id & 127
    pick = (iota((512, ROWS), 0) == id_hi).astype(F32).astype(BF16)
    table = home[...]
    table_hi = lax.shift_right_logical(table, 8).astype(F32).astype(BF16)
    table_lo = (table & 255).astype(F32).astype(BF16)
    lane = iota((128, ROWS), 0) == id_lo
    st_hi = jnp.sum(jnp.where(lane, tn(table_hi, pick), 0.0), axis=0, keepdims=True)
    st_lo = jnp.sum(jnp.where(lane, tn(table_lo, pick), 0.0), axis=0, keepdims=True)
    storage = st_hi.astype(I32) * 256 + st_lo.astype(I32)
    owner = lax.shift_right_logical(storage, 9)
    local = storage & 511
    match = (iota((OWN, ROWS), 0) == owner).astype(F32)
    before = (iota((ROWS, ROWS), 0) < iota((ROWS, ROWS), 1)).astype(F32).astype(BF16)
    earlier = nn(match.astype(BF16), before)
    position = jnp.sum(match * earlier, axis=0, keepdims=True).astype(I32)
    slot_s[...] = owner * CAP + position

    eye = (iota((128, M), 0) == iota((128, M), 1)).astype(F32).astype(BF16)
    turned = nt(eye, code_ids[...].astype(F32).astype(BF16))
    pcodes[...] = turned.astype(I32)
    line = iota((128, ROWS), 0)
    aux = jnp.where(line == 96, (lax.shift_right_logical(local, 8)).astype(F32), 0.0)
    aux = aux + jnp.where(line == 97, (local & 255).astype(F32), 0.0)
    aux = aux + jnp.where(line == 98, 1.0, 0.0)
    packed = (turned + aux).astype(BF16)

    def place(i):
        return (iota((128, ROWS), 0) + 128 * i == slot_s[...]).astype(F32).astype(BF16)

    def codes_chunk(i, _):
        block = nt(place(i), packed)
        scode[pl.ds(16 * i, 16)] = block.reshape(16, CAP, 128).astype(BF16)
        return 0

    lax.fori_loop(0, 8, codes_chunk, 0)

    def rows_chunk(i, _):
        block = nn(place(i), points[...])
        srow[pl.ds(16 * i, 16)] = block.reshape(16, CAP, D).astype(BF16)
        return 0

    lax.fori_loop(0, 8, rows_chunk, 0)

    pl.semaphore_wait(barrier, 17)
    for peer in line_x:
        pl.semaphore_signal(sem_a, inc=1, device_id=peer, device_id_type=MESH)
    pl.semaphore_wait(sem_a, 7)
    for peer in line_y:
        pl.semaphore_signal(sem_b, inc=1, device_id=peer, device_id_type=MESH)
    pl.semaphore_wait(sem_b, 3)

    def code_copy(k):
        to = me ^ k
        return pltpu.make_async_remote_copy(
            src_ref=scode.at[to], dst_ref=rcode.at[me], send_sem=code_send, recv_sem=code_recv,
            device_id={"own": to}, device_id_type=MESH)

    def send_code(k, _):
        code_copy(k).start()
        return 0

    lax.fori_loop(1, OWN, send_code, 0)

    def row_copy(to):
        return pltpu.make_async_remote_copy(
            src_ref=srow.at[to], dst_ref=rrow.at[me], send_sem=row_send,
            recv_sem=row_recv.at[zl], device_id={"own": to}, device_id_type=MESH)

    def send_row(k, _):
        row_copy(me ^ ((k % 4) * 32 + k // 4)).start()
        return 0

    lax.fori_loop(1, OWN, send_row, 0)
    rcode[me] = scode[me]
    rrow[me] = srow[me]

    def split(value, at_, cols):
        hi = value.astype(BF16)
        ehi[at_, cols] = hi
        elo[at_, cols] = (value - hi.astype(F32)).astype(BF16)

    for i in range(3):
        rows_i = pl.ds(256 * i, 256)
        split(tt(rotation[:, 256 * i:256 * i + 256], points[...]), rows_i, pl.ds(0, ROWS))
        part = -tt(rotation[:, 256 * i:256 * i + 256], centroids[...])
        hi = part.astype(BF16)
        crt_hi[rows_i, :] = hi
        crt_lo[rows_i, :] = (part - hi.astype(F32)).astype(BF16)

    def group(g, codes, n, with_counts):
        rhs, high = [], []
        for ml in range(4):
            code = codes[pl.ds(4 * g + ml, 1), pl.ds(0, n)]
            rhs.append((iota((64, n), 0) == (code & 63)).astype(F32).astype(BF16))
            wide = jnp.broadcast_to(code, (8, n))
            book = codebook[4 * g + ml].astype(F32)
            parts = []
            for b in range(n // 128):
                idx = wide[:, 128 * b:128 * b + 128]
                low_idx = idx & 127
                first = jnp.take_along_axis(book[:, :128], low_idx, axis=1)
                second = jnp.take_along_axis(book[:, 128:], low_idx, axis=1)
                parts.append(jnp.where(idx < 128, first, second))
            high.append(lax.shift_right_arithmetic(wide, 6))
            reb_rows = jnp.concatenate(parts, axis=1)
            high[-1] = (high[-1], reb_rows)
        reb[pl.ds(pl.multiple_of(32 * g, 32), 32), pl.ds(0, n)] = jnp.concatenate(
            [h[1] for h in high], axis=0).astype(BF16)
        upper = jnp.concatenate([h[0] for h in high], axis=0)
        rhs = jnp.concatenate(rhs, axis=0)
        rows_g = pl.ds(pl.multiple_of(32 * g, 32), 32)
        e1 = ehi[rows_g, pl.ds(0, n)].astype(F32)
        e2 = elo[rows_g, pl.ds(0, n)].astype(F32)
        masks = [upper == a for a in range(4)]
        lhs = [jnp.where(k, e1, 0.0).astype(BF16) for k in masks]
        lhs += [jnp.where(k, e2, 0.0).astype(BF16) for k in masks]
        if with_counts:
            lhs += [k.astype(F32).astype(BF16) for k in masks]
        out = nt(jnp.concatenate(lhs, axis=0), rhs)
        keep = (iota((32, 256), 0) // 8) == (iota((32, 256), 1) // 64)
        left = iota((32, 128), 1) < 64

        def fold(v):
            v = jnp.where(keep, v, 0.0)
            v = v[:, :128] + v[:, 128:]
            return v + pltpu.roll(v, 64, 1)

        s = [fold(out[32 * a:32 * a + 32] + out[128 + 32 * a:160 + 32 * a]) for a in range(4)]
        s_lo, s_hi = jnp.where(left, s[0], s[1]), jnp.where(left, s[2], s[3])
        if with_counts:
            k = [fold(out[256 + 32 * a:288 + 32 * a]) for a in range(4)]
            counts[rows_g, :] = jnp.concatenate(
                [jnp.where(left, k[0], k[1]), jnp.where(left, k[2], k[3])], axis=1)
            sums[rows_g, :] = jnp.concatenate([s_lo, s_hi], axis=1)
        else:
            sums[rows_g, :] += jnp.concatenate([s_lo, s_hi], axis=1)

    def own_group(g, _):
        group(g, pcodes, ROWS, True)
        return 0

    lax.fori_loop(0, M // 4, own_group, 0)
    for i in range(3):
        cols = pl.ds(256 * i, 256)
        gram[cols, :] = tt(points[:, 256 * i:256 * i + 256], reb[:, pl.ds(0, ROWS)])

    pltpu.make_async_copy(rcode.at[pl.ds(0, OWN - 1)], rcode.at[pl.ds(0, OWN - 1)], code_recv).wait()
    ident = (iota((128, 128), 0) == iota((128, 128), 1)).astype(F32).astype(BF16)
    got = nt(ident, rcode[...].astype(F32).reshape(SLOTS, 128).astype(BF16))
    ccodes[...] = got.astype(I32)
    here = got[96:97, :] * 256.0 + got[97:98, :] - 1024.0 * (1.0 - got[98:99, :])
    local_s[...] = here.astype(I32)
    onel[...] = (iota((512, SLOTS), 0) == local_s[...]).astype(F32).astype(BF16)
    for i in range(3):
        rows_i = pl.ds(256 * i, 256)
        ehi[rows_i, :] = nn(crt_hi[rows_i, :], onel[...]).astype(BF16)
        elo[rows_i, :] = nn(crt_lo[rows_i, :], onel[...]).astype(BF16)

    def got_group(g, _):
        group(g, ccodes, SLOTS, False)
        return 0

    lax.fori_loop(0, M // 4, got_group, 0)
    for i in range(3):
        cols = pl.ds(256 * i, 256)
        turned_c = tn(centroids[:, 256 * i:256 * i + 256], onel[...]).astype(BF16)
        gram[cols, :] -= nt(turned_c, reb[...])
    for i in range(4):
        centre[pl.ds(256 * i, 256), :] = tn(onel[:, 256 * i:256 * i + 256], centroids[...]).astype(BF16)

    state = [0]
    sent = []

    def remote(src, dst, peer):
        k = state[0]
        state[0] += 1
        copy = pltpu.make_async_remote_copy(
            src_ref=src, dst_ref=dst, send_sem=red_send.at[k], recv_sem=red_recv.at[k],
            device_id=peer, device_id_type=MESH)
        copy.start()
        sent.append(copy)
        return copy

    def arrive(copies):
        for copy in copies:
            copy.wait_recv()

    s0g[...] = gram[:, pl.ds(384 * other, 384)].reshape(16, Q, 384).astype(BF16)
    s0s[:, :, 0:128] = sums[:, pl.ds(128 * other, 128)].reshape(16, Q, 128).astype(BF16)
    s0s[:, :, 128:256] = counts[:, pl.ds(128 * other, 128)].reshape(16, Q, 128).astype(BF16)
    peer_c = at(z, y, x, other)
    copies = [remote(s0g, r0g, peer_c), remote(s0s, r0s, peer_c)]
    arrive(copies)
    mine_g = gram[:, pl.ds(384 * c, 384)].reshape(16, Q, 384)
    s1g[...] = (mine_g + r0g[...].astype(F32)).astype(BF16)
    mine_s = jnp.concatenate([sums[:, pl.ds(128 * c, 128)], counts[:, pl.ds(128 * c, 128)]], axis=1)
    s1s[...] = (mine_s.reshape(16, Q, 256) + r0s[...].astype(F32)).astype(BF16)

    copies = []
    for d in range(1, 4):
        x2, y2 = (x + d) % 4, (y + d) % 4
        copies.append(remote(s1g.at[pl.ds(4 * x2, 4)], r1g.at[d - 1], at(z, y, x2, c)))
        copies.append(remote(s1s.at[pl.ds(4 * y2, 4)], r1s.at[d - 1], at(z, y2, x, c)))
    arrive(copies)
    own_g = s1g[pl.ds(4 * x, 4)].astype(F32)
    own_s = s1s[pl.ds(4 * y, 4)].astype(F32)
    for d in range(3):
        own_g = own_g + r1g[d].astype(F32)
        own_s = own_s + r1s[d].astype(F32)
    s2g[...] = own_g.astype(BF16)
    s2s[...] = own_s.astype(BF16)

    copies = []
    for d in range(1, 4):
        x2, y2 = (x + d) % 4, (y + d) % 4
        copies.append(remote(s2g.at[y2], r2g.at[d - 1], at(z, y2, x, c)))
        copies.append(remote(s2s.at[x2], r2s.at[d - 1], at(z, y, x2, c)))
    arrive(copies)
    own_g = s2g[y].astype(F32)
    own_s = s2s[x].astype(F32)
    for d in range(3):
        own_g = own_g + r2g[d].astype(F32)
        own_s = own_s + r2s[d].astype(F32)
    for p in range(6):
        s3g[p] = own_g[24 * (p // 3):24 * (p // 3) + 24, 128 * (p % 3):128 * (p % 3) + 128]
    for p in range(2):
        s3s[p] = own_s[24 * p:24 * p + 24, :]

    base = state[0]

    def z_copy(d, is_gram):
        z2 = (z + d) % 8
        k = base + d - 1
        if is_gram:
            src, dst = s3g.at[jnp.minimum(z2, 5)], r3g.at[d - 1]
        else:
            src, dst = s3s.at[jnp.maximum(z2 - 6, 0)], r3s.at[d - 1]
        return pltpu.make_async_remote_copy(
            src_ref=src, dst_ref=dst, send_sem=red_send.at[k], recv_sem=red_recv.at[k],
            device_id=at(z2, y, x, c), device_id_type=MESH)

    for d in range(1, 8):
        z2 = (z + d) % 8

        @pl.when(z2 < 6)
        def _():
            z_copy(d, True).start()

        @pl.when(z2 >= 6)
        def _():
            z_copy(d, False).start()

    state[0] += 7

    @pl.when(z < 6)
    def _():
        total = s3g[jnp.minimum(z, 5)]
        for d in range(1, 8):
            z_copy(d, True).wait_recv()
            total = total + r3g[d - 1]
        fin[...] = total * (1.0 / math.sqrt(OWN * 2 * ROWS))

    @pl.when(z >= 6)
    def _():
        part = jnp.maximum(z - 6, 0)
        total = s3s[part]
        for d in range(1, 8):
            z_copy(d, False).wait_recv()
            total = total + r3s[d - 1]
        first = 6 * (4 * y + x) + 3 * part
        old = codebook[pl.ds(first, 3), :, pl.ds(128 * c, 128)].astype(F32).reshape(24, 128)
        fin[...] = (total[:, :128] + old) / (total[:, 128:] + 1.0)

    copies = [remote(fin, a4.at[z], at((z + d) % 8, y, x, c)) for d in range(1, 8)]
    a4[z] = fin[...]
    arrive(copies)
    a5g[y] = jnp.concatenate(
        [jnp.concatenate([a4[3 * h + k] for k in range(3)], axis=1) for h in range(2)], axis=0
    ).astype(BF16)
    a5s[x] = jnp.concatenate([a4[6], a4[7]], axis=0).astype(BF16)

    copies = []
    for d in range(1, 4):
        x2, y2 = (x + d) % 4, (y + d) % 4
        copies.append(remote(a5g.at[y], a5g.at[y], at(z, y2, x, c)))
        copies.append(remote(a5s.at[x], a5s.at[x], at(z, y, x2, c)))
    arrive(copies)
    a6g[pl.ds(4 * x, 4)] = a5g[...]
    a6s[pl.ds(4 * y, 4)] = a5s[...]
    copies = []
    for d in range(1, 4):
        x2, y2 = (x + d) % 4, (y + d) % 4
        copies.append(remote(a6g.at[pl.ds(4 * x, 4)], a6g.at[pl.ds(4 * x, 4)], at(z, y, x2, c)))
        copies.append(remote(a6s.at[pl.ds(4 * y, 4)], a6s.at[pl.ds(4 * y, 4)], at(z, y2, x, c)))
    arrive(copies)
    copies = [remote(a6g, a7g, peer_c), remote(a6s, a7s, peer_c)]
    gram_out[:, pl.ds(384 * c, 384)] = a6g[...].astype(F32).reshape(D, 384)
    book_out[:, :, pl.ds(128 * c, 128)] = a6s[...].astype(F32).reshape(M, 8, 128)

    for s in range(ROW_CHUNKS):
        blocks = pl.ds(32 * s, 32)

        @pl.when(zl == s)
        def _():
            pltpu.make_async_copy(
                rrow.at[pl.ds(0, 31)], rrow.at[pl.ds(0, 31)], row_recv.at[s]).wait()

        @pl.when(zl != s)
        def _():
            pltpu.make_async_copy(rrow.at[blocks], rrow.at[blocks], row_recv.at[s]).wait()

        rows_s = rrow[blocks].astype(F32).reshape(256, D)
        resid = (rows_s - centre[pl.ds(256 * s, 256), :].astype(F32)).astype(BF16)
        enc_out[pl.ds(256 * s, 256), :] = nn(resid, rotation[...]).astype(BF16)

    arrive(copies)
    gram_out[:, pl.ds(384 * other, 384)] = a7g[...].astype(F32).reshape(D, 384)
    book_out[:, :, pl.ds(128 * other, 128)] = a7s[...].astype(F32).reshape(M, 8, 128)
    for copy in sent:
        copy.wait_send()
    for d in range(1, 8):
        z2 = (z + d) % 8

        @pl.when(z2 < 6)
        def _():
            z_copy(d, True).wait_send()

        @pl.when(z2 >= 6)
        def _():
            z_copy(d, False).wait_send()

    pltpu.make_async_copy(scode.at[pl.ds(0, OWN - 1)], scode.at[pl.ds(0, OWN - 1)], code_send).wait()
    pltpu.make_async_copy(srow.at[pl.ds(0, OWN - 1)], srow.at[pl.ds(0, OWN - 1)], row_send).wait()


def shards(points, list_ids, code_ids, list_home, centroids, rotation, codebook):
    vmem = pl.BlockSpec(memory_space=pltpu.VMEM)
    scratch = [
        ((OWN, CAP, D), BF16), ((OWN, CAP, D), BF16), ((OWN, CAP, 128), BF16), ((OWN, CAP, 128), BF16),
        ((1, ROWS), I32), ((128, ROWS), I32), ((128, SLOTS), I32),
        ((D, SLOTS), BF16), ((D, SLOTS), BF16), ((D, SLOTS), BF16), ((D, 512), BF16), ((D, 512), BF16),
        ((SLOTS, D), BF16), ((512, SLOTS), BF16), ((1, SLOTS), I32),
        ((D, D), F32), ((D, 256), F32), ((D, 256), F32),
        ((16, Q, 384), BF16), ((16, Q, 256), BF16), ((16, Q, 384), BF16), ((16, Q, 256), BF16),
        ((16, Q, 384), BF16), ((16, Q, 256), BF16), ((3, 4, Q, 384), BF16), ((3, 4, Q, 256), BF16),
        ((4, Q, 384), BF16), ((4, Q, 256), BF16), ((3, Q, 384), BF16), ((3, Q, 256), BF16),
        ((6, 24, 128), F32), ((2, 24, 256), F32), ((7, 24, 128), F32), ((7, 24, 256), F32),
        ((24, 128), F32), ((8, 24, 128), F32), ((4, Q, 384), BF16), ((4, Q, 128), BF16),
        ((16, Q, 384), BF16), ((16, Q, 128), BF16), ((16, Q, 384), BF16), ((16, Q, 128), BF16),
    ]
    dma = pltpu.SemaphoreType.DMA
    encoded, book, gram = pl.pallas_call(
        kernel,
        out_shape=(
            jax.ShapeDtypeStruct((SLOTS, D), BF16),
            jax.ShapeDtypeStruct((M, 8, 256), F32),
            jax.ShapeDtypeStruct((D, D), F32),
        ),
        in_specs=[vmem] * 7,
        out_specs=(vmem, vmem, vmem),
        scratch_shapes=[pltpu.VMEM(s, t) for s, t in scratch] + [
            dma, dma, dma, dma((ROW_CHUNKS,)), dma((42,)), dma((42,)),
            pltpu.SemaphoreType.REGULAR, pltpu.SemaphoreType.REGULAR, dma,
        ],
        compiler_params=pltpu.CompilerParams(
            collective_id=0, has_side_effects=True, vmem_limit_bytes=60 * 2**20),
    )(
        points, list_ids.reshape(1, ROWS), code_ids, list_home.reshape(512, 128),
        centroids, rotation, codebook,
    )
    return encoded, book, gram


def solution(mesh):
    return jax.shard_map(
        shards,
        mesh=mesh,
        in_specs=(
            P(("grp", "own"), None),
            P(("grp", "own")),
            P(("grp", "own"), None),
            P(),
            P("own", None),
            P(),
            P(),
        ),
        out_specs=(P(("grp", "own"), None), P(), P()),
        check_vma=False,
    )
```

```python
import math

import jax
import jax.numpy as jnp
from jax import lax
from jax.experimental import pallas as pl
from jax.experimental.pallas import tpu as pltpu
from jax.sharding import PartitionSpec as P

MESH = pl.DeviceIdType.MESH
F32 = jnp.float32
BF16 = jnp.bfloat16
I32 = jnp.int32

NZ, NY, NX = 8, 4, 4
OWN = 128
CAP = 8
ROWS = 512
D = 768
M = 96
SLOTS = OWN * CAP
Q = 48
ROW_CHUNKS = 4
UNROLL = 8
CHAINS = 4


def dot(a, b, dims):
    return lax.dot_general(a, b, (dims, ((), ())), preferred_element_type=F32)


def nn(a, b):
    return dot(a, b, ((1,), (0,)))


def nt(a, b):
    return dot(a, b, ((1,), (1,)))


def tn(a, b):
    return dot(a, b, ((0,), (0,)))


def tt(a, b):
    return dot(a, b, ((0,), (1,)))


def iota(shape, axis):
    return lax.broadcasted_iota(I32, shape, axis)


def kernel(
    points_h, ids_h, codes_h, home_h, centroids_h, rotation_h, codebook_h,
    resid_h, tiles_h,
    pc, ids, code_ids, home, rotation, codebook, rot_t, where_s, resid,
    srow, rrow, scode, rcode, slot_s, ccodes, ehi, elo, reb, crt_hi, crt_lo,
    centre, onel, local_s, gram, sums, counts,
    turned_c, g0s, g0r, g1s, g1r, c0s, c0r, c1s, c1r, gzs, gzr, czs, czr, a4, a6, a7,
    code_send, code_recv, row_send, row_recv, red_send, red_recv, z_send, z_recv, a_send, a_recv, sem_a, sem_b, load_sem, out_sem,
):
    points, centroids = pc.at[pl.ds(0, ROWS)], pc.at[pl.ds(ROWS, ROWS)]
    loads = [
        pltpu.make_async_copy(src, dst, load_sem.at[k])
        for k, (src, dst) in enumerate((
            (ids_h, ids), (home_h, home), (codes_h, code_ids), (points_h, points),
            (rotation_h, rotation), (centroids_h, centroids), (codebook_h, codebook)))
    ]
    for load in loads:
        load.start()
    me = lax.axis_index("own")
    z = lax.axis_index("grp") * 4 + me // 32
    zl = me // 32
    y = (me // 8) % 4
    x = (me // 2) % 4
    c = me % 2
    other = 1 - c

    def at(z_, y_, x_, c_):
        return {"grp": z_ // 4, "own": (z_ % 4) * 32 + y_ * 8 + x_ * 2 + c_}

    line_x = [at(z, y, (x + d) % 4, (c + e) % 2) for d in range(4) for e in range(2) if d or e]
    line_y = [at(z, (y + d) % 4, x, c) for d in range(1, 4)]
    line_z = [at((z + d) % 8, y, x, c) for d in range(1, 8)]
    barrier = pltpu.get_barrier_semaphore()
    for peer in line_x + line_y + line_z:
        pl.semaphore_signal(barrier, inc=1, device_id=peer, device_id_type=MESH)

    loads[0].wait()
    loads[1].wait()
    row_id = ids[...]
    id_hi = lax.shift_right_logical(row_id, 7)
    id_lo = row_id & 127
    pick = (iota((512, ROWS), 0) == id_hi).astype(F32).astype(BF16)
    table = home[...]
    table_hi = lax.shift_right_logical(table, 8).astype(F32).astype(BF16)
    table_lo = (table & 255).astype(F32).astype(BF16)
    lane = iota((128, ROWS), 0) == id_lo
    st_hi = jnp.sum(jnp.where(lane, tn(table_hi, pick), 0.0), axis=0, keepdims=True)
    st_lo = jnp.sum(jnp.where(lane, tn(table_lo, pick), 0.0), axis=0, keepdims=True)
    storage = st_hi.astype(I32) * 256 + st_lo.astype(I32)
    owner = lax.shift_right_logical(storage, 9)
    local = storage & 511
    match = (iota((OWN, ROWS), 0) == owner).astype(F32)
    before = (iota((ROWS, ROWS), 0) < iota((ROWS, ROWS), 1)).astype(F32).astype(BF16)
    earlier = nn(match.astype(BF16), before)
    position = jnp.sum(match * earlier, axis=0, keepdims=True).astype(I32)
    slot_s[...] = owner * CAP + position

    loads[2].wait()
    pl.semaphore_wait(barrier, 17)
    for peer in line_x:
        pl.semaphore_signal(sem_a, inc=1, device_id=peer, device_id_type=MESH)
    line = iota((32, ROWS), 0)
    aux = jnp.where(line == 0, (lax.shift_right_logical(local, 8)).astype(F32), 0.0)
    aux = aux + jnp.where(line == 1, (local & 255).astype(F32), 0.0)
    aux = aux + jnp.where(line == 2, 1.0, 0.0)
    packed = jnp.concatenate([code_ids[...].astype(F32), aux], axis=0).astype(BF16)

    def code_copy(to):
        return pltpu.make_async_remote_copy(
            src_ref=scode.at[to], dst_ref=rcode.at[me], send_sem=code_send, recv_sem=code_recv,
            device_id={"own": to}, device_id_type=MESH)

    def row_copy(to):
        return pltpu.make_async_remote_copy(
            src_ref=srow.at[to], dst_ref=rrow.at[me], send_sem=row_send,
            recv_sem=row_recv.at[zl], device_id={"own": to}, device_id_type=MESH)

    order = (4, 6, 2, 5, 7, 3, 1, 0)
    for i in order:
        j = (me // 16) ^ i
        there = (iota((128, ROWS), 0) + 128 * j == slot_s[...]).astype(F32).astype(BF16)
        where_s[pl.ds(pl.multiple_of(128 * j, 128), 128), :] = there
        scode[pl.ds(16 * j, 16)] = nt(there, packed).reshape(16, CAP, 128).astype(BF16)
    pl.semaphore_wait(sem_a, 7)
    for peer in line_y:
        pl.semaphore_signal(sem_b, inc=1, device_id=peer, device_id_type=MESH)
    loads[4].wait()
    rot_t[...] = rotation[...].T
    pl.semaphore_wait(sem_b, 3)
    for i in order:
        for k in range(16):
            if i or k:
                code_copy(me ^ (16 * i + k)).start()
    loads[3].wait()
    for i in order:
        j = (me // 16) ^ i
        block = nn(where_s[pl.ds(pl.multiple_of(128 * j, 128), 128), :], points[...])
        srow[pl.ds(16 * j, 16)] = block.reshape(16, CAP, D).astype(BF16)

    def send_rows(first, last):
        for k in range(first, last):
            row_copy(me ^ ((k % 4) * 32 + k // 4)).start()

    send_rows(1, OWN)
    rcode[me] = scode[me]
    rrow[me] = srow[me]

    def split(value, at_, cols):
        hi = value.astype(BF16)
        ehi[at_, cols] = hi
        elo[at_, cols] = (value - hi.astype(F32)).astype(BF16)

    loads[5].wait()
    loads[6].wait()
    for i in range(3):
        rows_i = pl.ds(256 * i, 256)
        both = nt(rot_t[rows_i, :], pc[...])
        split(both[:, :ROWS], rows_i, pl.ds(0, ROWS))
        part = -both[:, ROWS:]
        hi = part.astype(BF16)
        crt_hi[rows_i, :] = hi
        crt_lo[rows_i, :] = (part - hi.astype(F32)).astype(BF16)

    def rebuild(g, codes, n):
        rebuilt = []
        for ml in range(4):
            wide = jnp.broadcast_to(codes[pl.ds(4 * g + ml, 1), pl.ds(0, n)], (8, n))
            book = codebook[4 * g + ml].astype(F32)
            parts = []
            for b in range(n // 128):
                idx = wide[:, 128 * b:128 * b + 128]
                low_idx = idx & 127
                first = jnp.take_along_axis(book[:, :128], low_idx, axis=1)
                second = jnp.take_along_axis(book[:, 128:], low_idx, axis=1)
                parts.append(jnp.where(idx < 128, first, second))
            rebuilt.append(jnp.concatenate(parts, axis=1))
        rows_g = pl.ds(pl.multiple_of(32 * g, 32), 32)
        reb[rows_g, pl.ds(0, n)] = jnp.concatenate(rebuilt, axis=0).astype(BF16)

    def group(g, codes, n, with_counts):
        rows_g = pl.ds(pl.multiple_of(32 * g, 32), 32)
        rhs, high = [], []
        steps = iota((16, n), 0).astype(F32).astype(BF16)
        one, zero = jnp.ones((16, n), BF16), jnp.zeros((16, n), BF16)
        for ml in range(4):
            wide = jnp.broadcast_to(codes[pl.ds(4 * g + ml, 1), pl.ds(0, n)], (8, n))
            low = (jnp.concatenate([wide, wide], axis=0) & 63).astype(F32).astype(BF16)
            rhs += [jnp.where(low == steps + jnp.asarray(16 * k, BF16), one, zero) for k in range(4)]
            high.append(lax.shift_right_arithmetic(wide, 6).astype(F32))
        upper = jnp.concatenate(high, axis=0).astype(BF16)
        e1, e2 = ehi[rows_g, pl.ds(0, n)], elo[rows_g, pl.ds(0, n)]
        none = jnp.zeros((32, n), BF16)
        masks = [upper == jnp.asarray(a, BF16) for a in range(4)]
        lhs = [jnp.where(k, e1, none) for k in masks] + [jnp.where(k, e2, none) for k in masks]
        if with_counts:
            rows_8 = pl.ds(pl.multiple_of(8 * (g // 2), 8), 8)
            of_8 = lax.shift_right_arithmetic(codes[rows_8, pl.ds(0, n)], 6)
            lhs.append(jnp.concatenate(
                [(of_8 == a).astype(F32) for a in range(4)], axis=0).astype(BF16))
        out = nt(jnp.concatenate(lhs, axis=0), jnp.concatenate(rhs, axis=0))
        left32, left8 = iota((32, 128), 1) < 64, iota((8, 128), 1) < 64

        def fold(v, keep):
            v = jnp.where(keep, v, 0.0)
            v = v[:, :128] + v[:, 128:]
            return v + pltpu.roll(v, 64, 1)

        keep = (iota((32, 256), 0) // 8) == (iota((32, 256), 1) // 64)
        s = [fold(out[32 * a:32 * a + 32] + out[128 + 32 * a:160 + 32 * a], keep) for a in range(4)]
        s = jnp.concatenate(
            [jnp.where(left32, s[0], s[1]), jnp.where(left32, s[2], s[3])], axis=1)
        if with_counts:
            sums[rows_g, :] = s
            keep = iota((8, 256), 0) == 4 * (g % 2) + iota((8, 256), 1) // 64
            k = [fold(out[256 + 8 * a:264 + 8 * a], keep) for a in range(4)]
            counts[rows_8, :] += jnp.concatenate(
                [jnp.where(left8, k[0], k[1]), jnp.where(left8, k[2], k[3])], axis=1)
        else:
            sums[rows_g, :] += s

    counts[...] = jnp.zeros_like(counts)

    def own_group(g, _):
        rebuild(g, code_ids, ROWS)
        group(g, code_ids, ROWS, True)
        return 0

    lax.fori_loop(0, M // 4, own_group, 0, unroll=UNROLL)
    for i in range(3):
        cols = pl.ds(256 * i, 256)
        gram[cols, :] = tt(points[:, 256 * i:256 * i + 256], reb[:, pl.ds(0, ROWS)])

    pltpu.make_async_copy(rcode.at[pl.ds(0, OWN - 1)], rcode.at[pl.ds(0, OWN - 1)], code_recv).wait()
    ident = (iota((128, 128), 0) == iota((128, 128), 1)).astype(F32).astype(BF16)
    got = nt(ident, rcode[...].astype(F32).reshape(SLOTS, 128).astype(BF16))
    ccodes[...] = got.astype(I32)
    here = got[96:97, :] * 256.0 + got[97:98, :] - 1024.0 * (1.0 - got[98:99, :])
    local_s[...] = here.astype(I32)
    onel[...] = (iota((512, SLOTS), 0) == local_s[...]).astype(F32).astype(BF16)

    for i in range(3):
        rows_i = pl.ds(256 * i, 256)
        turned_c[rows_i, :] = tn(centroids[:, 256 * i:256 * i + 256], onel[...]).astype(BF16)

    state = [0]
    sent = []
    q = 4 * x + y
    peer_c = at(z, y, x, other)

    def remote(src, dst, peer):
        k = state[0]
        state[0] += 1
        copy = pltpu.make_async_remote_copy(
            src_ref=src, dst_ref=dst, send_sem=red_send.at[k], recv_sem=red_recv.at[k],
            device_id=peer, device_id_type=MESH)
        copy.start()
        sent.append(copy)
        return copy

    def arrive(copies):
        for copy in copies:
            copy.wait_recv()

    def in_plane(d):
        q2 = q ^ d
        return q2, at(z, q2 % 4, q2 // 4, c)

    def counted(value):
        top = value.astype(BF16).astype(F32)
        return jnp.concatenate([top, value - top], axis=-2)

    def tiles(j, half):
        if j < 3:
            return gram[:, pl.ds(128 * (2 * j + half), 128)].reshape(16, 3, 16, 128)
        cols = pl.ds(128 * half, 128)
        rows_8 = jnp.stack([counts[6 * b:6 * b + 8, cols] for b in range(16)])
        return jnp.concatenate(
            [sums[:, cols].reshape(16, 3, 16, 128), counted(rows_8)[:, None]], axis=1)

    def settle(j, value):
        if j < 3:
            return value.astype(BF16)
        both = value[..., 3, :8, :] + value[..., 3, 8:, :]
        return jnp.concatenate(
            [value[..., :3, :, :], counted(both)[..., None, :, :]], axis=-3).astype(BF16)

    core_s = [g0s.at[0], g0s.at[1], g0s.at[2], c0s]
    core_r = [g0r.at[0], g0r.at[1], g0r.at[2], c0r]
    plane_s = [g1s.at[0], g1s.at[1], g1s.at[2], c1s]
    plane_r = [g1r.at[0], g1r.at[1], g1r.at[2], c1r]
    line_s = [gzs.at[0], gzs.at[1], gzs.at[2], czs]
    line_r = [gzr.at[0], gzr.at[1], gzr.at[2], czr]
    flight = {}

    def owner_z(j, r):
        return (3 * j + r) % 8

    def z_copy(j, r):
        to = owner_z(j, r)
        slot = jnp.maximum((z ^ to) - 1, 0)
        return pltpu.make_async_remote_copy(
            src_ref=line_s[j].at[r], dst_ref=line_r[j].at[slot], send_sem=z_send.at[j, r],
            recv_sem=z_recv.at[j, slot], device_id=at(jnp.int32(to), y, x, c), device_id_type=MESH)

    def z_arrival(j, r, d):
        return pltpu.make_async_remote_copy(
            src_ref=line_s[j].at[r], dst_ref=line_r[j].at[d - 1], send_sem=z_send.at[j, r],
            recv_sem=z_recv.at[j, d - 1], device_id=at(z ^ d, y, x, c), device_id_type=MESH)

    def back_copy(j, r, d):
        return pltpu.make_async_remote_copy(
            src_ref=a4.at[j, r], dst_ref=a4.at[j, r], send_sem=a_send.at[j, d - 1],
            recv_sem=a_recv.at[j, r], device_id=at(z ^ d, y, x, c), device_id_type=MESH)

    def to_core(j):
        core_s[j][...] = tiles(j, other).astype(BF16)
        flight["core", j] = [remote(core_s[j], core_r[j], peer_c)]

    def to_plane(j):
        arrive(flight["core", j])
        plane_s[j][...] = settle(j, tiles(j, c) + core_r[j][...].astype(F32))
        flight["plane", j] = []
        for d in range(1, 16):
            q2, peer = in_plane(d)
            flight["plane", j].append(remote(plane_s[j].at[q2], plane_r[j].at[d - 1], peer))

    def to_line(j):
        arrive(flight["plane", j])
        value = plane_s[j][q].astype(F32)
        for d in range(15):
            value = value + plane_r[j][d].astype(F32)
        value = settle(j, value)
        for r in range(3):
            line_s[j][r, 0] = value[r]
            if j == 3:
                line_s[j][r, 1] = value[3]

            @pl.when(z != owner_z(j, r))
            def _():
                z_copy(j, r).start()

    def finish_line(j):
        for r in range(3):
            @pl.when(z == owner_z(j, r))
            def _():
                total = line_s[j][r].astype(F32)
                for d in range(1, 8):
                    z_arrival(j, r, d).wait_recv()
                    total = total + line_r[j][d - 1].astype(F32)
                if j < 3:
                    a4[j, r] = (total[0] * (1.0 / math.sqrt(OWN * 2 * ROWS))).astype(BF16)
                else:
                    count = total[1, :8] + total[1, 8:]
                    count = jnp.concatenate([
                        jnp.broadcast_to(count[2 * r + k:2 * r + k + 1], (8, 128))
                        for k in range(2)], axis=0)
                    old = codebook[pl.ds(6 * q + 2 * r, 2), :, pl.ds(128 * c, 128)]
                    old = old.astype(F32).reshape(16, 128)
                    a4[j, r] = ((total[0] + old) / (count + 1.0)).astype(BF16)
                for d in range(1, 8):
                    back_copy(j, r, d).start()

    def back_plane(j):
        for r in range(3):
            @pl.when(z != owner_z(j, r))
            def _():
                back_copy(j, r, 1).wait_recv()
        a6[j, q] = a4[j]
        flight["back", j] = []
        for d in range(1, 16):
            q2, peer = in_plane(d)
            flight["back", j].append(remote(a6.at[j, q], a6.at[j, q], peer))

    outs = []

    def write(src, dst):
        out = pltpu.make_async_copy(src, dst, out_sem.at[len(outs)])
        out.start()
        outs.append(out)

    def back_core(j):
        arrive(flight["back", j])
        flight["last", j] = [remote(a6.at[j], a7.at[j], peer_c)]
        write(a6.at[j], tiles_h.at[c, j])

    def done(j):
        arrive(flight["last", j])
        write(a7.at[j], tiles_h.at[other, j])

    def got_groups(first, last):
        def got_group(g, _):
            group(g, ccodes, SLOTS, False)
            return 0

        lax.fori_loop(first, last, got_group, 0, unroll=UNROLL)

    def got_rebuild(g, _):
        rebuild(g, ccodes, SLOTS)
        return 0

    for j in range(3):
        lax.fori_loop(8 * j, 8 * j + 8, got_rebuild, 0, unroll=UNROLL)
        cols = pl.ds(256 * j, 256)
        gram[:, cols] -= nt(turned_c[...], reb[cols, :])
        to_core(j)
        if j:
            to_plane(j - 1)
    for i in range(3):
        rows_i = pl.ds(256 * i, 256)
        ehi[rows_i, :] = nn(crt_hi[rows_i, :], onel[...]).astype(BF16)
        elo[rows_i, :] = nn(crt_lo[rows_i, :], onel[...]).astype(BF16)
    to_plane(2)
    got_groups(0, 8)
    got_groups(8, 16)
    to_line(0)
    got_groups(16, 24)
    to_core(3)
    to_line(1)
    for i in range(4):
        centre[pl.ds(256 * i, 256), :] = tn(onel[:, 256 * i:256 * i + 256], centroids[...]).astype(BF16)
    to_plane(3)
    finish_line(0)
    to_line(2)
    finish_line(1)
    back_plane(0)
    finish_line(2)
    back_plane(1)
    to_line(3)
    back_plane(2)
    finish_line(3)
    back_core(0)
    back_core(1)
    back_plane(3)
    back_core(2)
    done(0)
    done(1)
    back_core(3)

    for s in range(ROW_CHUNKS):
        blocks = pl.ds(32 * s, 32)

        @pl.when(zl == s)
        def _():
            pltpu.make_async_copy(
                rrow.at[pl.ds(0, 31)], rrow.at[pl.ds(0, 31)], row_recv.at[s]).wait()

        @pl.when(zl != s)
        def _():
            pltpu.make_async_copy(rrow.at[blocks], rrow.at[blocks], row_recv.at[s]).wait()

        rows_s = rrow[blocks].astype(F32).reshape(256, D)
        part = pl.ds(256 * s, 256)
        resid[part, :] = (rows_s - centre[part, :].astype(F32)).astype(BF16)
        write(resid.at[part], resid_h.at[part])

    done(2)
    done(3)
    for out in outs:
        out.wait()
    for copy in sent:
        copy.wait_send()
    for j in range(CHAINS):
        for r in range(3):
            @pl.when(z != owner_z(j, r))
            def _():
                z_copy(j, r).wait_send()

            @pl.when(z == owner_z(j, r))
            def _():
                for d in range(1, 8):
                    back_copy(j, r, d).wait_send()
    pltpu.make_async_copy(scode.at[pl.ds(0, OWN - 1)], scode.at[pl.ds(0, OWN - 1)], code_send).wait()
    pltpu.make_async_copy(srow.at[pl.ds(0, OWN - 1)], srow.at[pl.ds(0, OWN - 1)], row_send).wait()


def finish(resid, rotation, tiles, enc_out, gram_out, book_out):
    enc_out[...] = nn(resid[...], rotation[...]).astype(BF16)
    for h in range(2):
        for b in range(tiles.shape[2]):
            for r in range(3):
                rows_r = slice(Q * b + 16 * r, Q * b + 16 * r + 16)
                for j in range(3):
                    first = 128 * (2 * j + h)
                    gram_out[rows_r, first:first + 128] = tiles[h, j, b, r].astype(F32)
                book_out[rows_r, 128 * h:128 * h + 128] = tiles[h, 3, b, r].astype(F32)


def shards(points, list_ids, code_ids, list_home, centroids, rotation, codebook):
    hbm = pl.BlockSpec(memory_space=pl.ANY)
    scratch = [
        ((2 * ROWS, D), BF16), ((1, ROWS), I32), ((M, ROWS), I32), ((512, 128), I32), ((D, D), BF16),
        ((M, 8, 256), BF16), ((D, D), BF16), ((SLOTS, ROWS), BF16), ((SLOTS, D), BF16),
        ((OWN, CAP, D), BF16), ((OWN, CAP, D), BF16), ((OWN, CAP, 128), BF16), ((OWN, CAP, 128), BF16),
        ((1, ROWS), I32), ((128, SLOTS), I32),
        ((D, SLOTS), BF16), ((D, SLOTS), BF16), ((D, SLOTS), BF16), ((D, 512), BF16), ((D, 512), BF16),
        ((SLOTS, D), BF16), ((512, SLOTS), BF16), ((1, SLOTS), I32),
        ((D, D), F32), ((D, 256), F32), ((M + 8, 256), F32),
        ((D, SLOTS), BF16),
        ((3, 16, 3, 16, 128), BF16), ((3, 16, 3, 16, 128), BF16),
        ((3, 16, 3, 16, 128), BF16), ((3, 15, 3, 16, 128), BF16),
        ((16, 4, 16, 128), BF16), ((16, 4, 16, 128), BF16),
        ((16, 4, 16, 128), BF16), ((15, 4, 16, 128), BF16),
        ((3, 3, 1, 16, 128), BF16), ((3, 7, 1, 16, 128), BF16),
        ((3, 2, 16, 128), BF16), ((7, 2, 16, 128), BF16),
        ((4, 3, 16, 128), BF16), ((4, 16, 3, 16, 128), BF16), ((4, 16, 3, 16, 128), BF16),
    ]
    dma = pltpu.SemaphoreType.DMA
    resid, tiles = pl.pallas_call(
        kernel,
        out_shape=(
            jax.ShapeDtypeStruct((SLOTS, D), BF16),
            jax.ShapeDtypeStruct((2, CHAINS, 16, 3, 16, 128), BF16),
        ),
        in_specs=[hbm] * 7,
        out_specs=(hbm,) * 2,
        scratch_shapes=[pltpu.VMEM(s, t) for s, t in scratch] + [
            dma, dma, dma, dma((ROW_CHUNKS,)), dma((128,)), dma((128,)),
            dma((4, 3)), dma((4, 7)), dma((4, 7)), dma((4, 3)),
            pltpu.SemaphoreType.REGULAR, pltpu.SemaphoreType.REGULAR, dma((7,)), dma((12,)),
        ],
        compiler_params=pltpu.CompilerParams(
            collective_id=0, has_side_effects=True, vmem_limit_bytes=60 * 2**20),
    )(
        points, list_ids.reshape(1, ROWS), code_ids.T, list_home.reshape(512, 128),
        centroids, rotation, codebook,
    )
    steps = 4
    encoded, gram, book = pl.pallas_call(
        finish,
        grid=(steps,),
        out_shape=(
            jax.ShapeDtypeStruct((SLOTS, D), BF16),
            jax.ShapeDtypeStruct((D, D), F32),
            jax.ShapeDtypeStruct((D, 256), F32),
        ),
        in_specs=[
            pl.BlockSpec((SLOTS // steps, D), lambda i: (i, 0)),
            pl.BlockSpec((D, D), lambda i: (0, 0)),
            pl.BlockSpec((2, CHAINS, 16 // steps, 3, 16, 128), lambda i: (0, 0, i, 0, 0, 0)),
        ],
        out_specs=(
            pl.BlockSpec((SLOTS // steps, D), lambda i: (i, 0)),
            pl.BlockSpec((D // steps, D), lambda i: (i, 0)),
            pl.BlockSpec((D // steps, 256), lambda i: (i, 0)),
        ),
        compiler_params=pltpu.CompilerParams(vmem_limit_bytes=60 * 2**20),
    )(resid, rotation, tiles)
    return encoded, book.reshape(M, 8, 256), gram


def solution(mesh):
    return jax.shard_map(
        shards,
        mesh=mesh,
        in_specs=(
            P(("grp", "own"), None),
            P(("grp", "own")),
            P(("grp", "own"), None),
            P(),
            P("own", None),
            P(),
            P(),
        ),
        out_specs=(P(("grp", "own"), None), P(), P()),
        check_vma=False,
    )
```
